128 devices in a mesh: fsdp: 8 (over x, core), ctx: 2 (over y_lo), tp: 8 (over z, y_hi).
Axes of the slice: x: 4, y: 4 (y_hi: 2, y_lo: 2; y = y_hi * 2 + y_lo), z: 4, core: 2. Of those that a mesh axis runs over, the one named last changes fastest.
Arguments:
- tokens: bfloat16 [16, 1024, 1536], P('fsdp', ('ctx', 'tp')), may hold values from -6 to 6
- positions: int32 [16, 1024], P('fsdp'), may hold values from 0 to 1023, each once within a row
- w_query: bfloat16 [1536, 1536], P(('fsdp', 'ctx'), 'tp'), may hold values from -0.15625 to 0.15625
- w_key: bfloat16 [1536, 768], P(('fsdp', 'ctx'), 'tp'), may hold values from -0.15625 to 0.15625
- w_value: bfloat16 [1536, 768], P(('fsdp', 'ctx'), 'tp'), may hold values from -0.15625 to 0.15625
- w_out: bfloat16 [1536, 1536], P('tp', ('fsdp', 'ctx')), may hold values from -0.875 to 0.875
- w_gate: bfloat16 [1536, 4096], P(('fsdp', 'ctx'), 'tp'), may hold values from -0.15625 to 0.15625
- w_up: bfloat16 [1536, 4096], P(('fsdp', 'ctx'), 'tp'), may hold values from -0.15625 to 0.15625
- down_weight: bfloat16 [4096, 1536], P('tp', ('fsdp', 'ctx')), may hold values from -0.09375 to 0.09375
- gain_attn: float32 [1536], replicated, may hold values from 0.1 to 1.9
- gain_mlp: float32 [1536], replicated, may hold values from 0.1 to 1.9
- cotangent: bfloat16 [16, 1024, 1536], P('fsdp', ('ctx', 'tp')), may hold values from -6 to 6
Outputs:
- output: bfloat16 [16, 1024, 1536], P('fsdp', ('ctx', 'tp'))
- grad_tokens: bfloat16 [16, 1024, 1536], P('fsdp', ('ctx', 'tp'))
- grad_query_w: float32 [1536, 1536], P(('fsdp', 'ctx'), 'tp')
- grad_key_w: float32 [1536, 768], P(('fsdp', 'ctx'), 'tp')
- grad_value_w: float32 [1536, 768], P(('fsdp', 'ctx'), 'tp')
- grad_out_w: float32 [1536, 1536], P('tp', ('fsdp', 'ctx'))
- grad_gate_w: float32 [1536, 4096], P(('fsdp', 'ctx'), 'tp')
- grad_up_w: float32 [1536, 4096], P(('fsdp', 'ctx'), 'tp')
- grad_down_w: float32 [4096, 1536], P('tp', ('fsdp', 'ctx'))
- grad_gain_attn: float32 [1536], replicated
- grad_gain_mlp: float32 [1536], replicated
The draws below stay inside these ranges and needn't reach their ends.
Inputs may be any that keep to these rules, and one draw needn't show every extreme that they name: `positions`: each row holds every number of 0 to 1023 once.
All inputs are finite; a program needn't handle non-finite values.
Results may differ from the reference program's by a relative error of at most 0.025.
Values may be sent and summed in bfloat16 or wider, within the bound.
No kernel may reach another device: no remote copies, remote signals or barrier semaphores. Data moves between devices by JAX's collectives and lax.ppermute only.
A program may use at most 128 MiB of HBM per device.

```python
import jax
import jax.numpy as jnp
from jax import lax

D = 1536
HQ = 16
KVH = 8
HD = 96
FF = 4096
LEN = 1024
SEQS = 16


def level_of(own_key, shape, cuts, least, top_value):
    def one(position, blocks):
        steps = jax.random.uniform(jax.random.fold_in(jax.random.fold_in(own_key, 6), position), (blocks,), jnp.float32, least / len(cuts), top_value / len(cuts))
        return jnp.repeat(jnp.exp(steps), shape[position] // blocks).reshape((-1,) + (1,) * (len(shape) - position - 1))

    factor_of = one(*cuts[0])
    for cut in cuts[1:]:
        factor_of = factor_of * one(*cut)
    return factor_of


def normal_values(own_key, dims, width, limit, split=(), dtype=jnp.bfloat16):
    gain = level_of(own_key, dims, split, -0.22, 0.18) if split else 1.0
    result = jax.random.normal(own_key, dims, jnp.float32) * width * gain
    return jnp.minimum(jnp.maximum(result, -limit), limit).astype(dtype)


def setup_inputs(seed: int = 0) -> dict:
    key_list = jax.random.split(jax.random.key(seed), 13)
    tokens = normal_values(key_list[0], (SEQS, LEN, D), 1.0, 6.0, ((0, 8), (1, 16)))
    positions = jax.vmap(lambda own: jax.random.permutation(own, LEN))(jax.random.split(key_list[1], SEQS)).reshape((SEQS, LEN)).astype(jnp.int32)
    w_query = normal_values(key_list[2], (D, HQ * HD), D ** -0.5, 0.15625, ((0, 16), (1, 8)))
    w_key = normal_values(key_list[3], (D, KVH * HD), D ** -0.5, 0.15625, ((0, 16), (1, 8)))
    w_value = normal_values(key_list[4], (D, KVH * HD), D ** -0.5, 0.15625, ((0, 16), (1, 8)))
    w_out = normal_values(key_list[5], (HQ * HD, D), (HD // 2) ** -0.5, 0.875, ((0, 8), (1, 16)))
    w_gate = normal_values(key_list[6], (D, FF), D ** -0.5, 0.15625, ((0, 16), (1, 8)))
    w_up = normal_values(key_list[7], (D, FF), D ** -0.5, 0.15625, ((0, 16), (1, 8)))
    down_weight = normal_values(key_list[8], (FF, D), FF ** -0.5, 0.09375, ((0, 8), (1, 16)))
    gain_attn = jnp.clip(1.0 + 0.18 * jax.random.normal(key_list[9], (D,), jnp.float32), 0.1, 1.9)
    gain_mlp = jnp.clip(1.0 + 0.18 * jax.random.normal(key_list[10], (D,), jnp.float32), 0.1, 1.9)
    cotangent = normal_values(key_list[11], (SEQS, LEN, D), 1.0, 6.0, ((0, 8), (1, 16)))
    return {"tokens": tokens, "positions": positions, "w_query": w_query, "w_key": w_key, "w_value": w_value, "w_out": w_out, "w_gate": w_gate, "w_up": w_up, "down_weight": down_weight, "gain_attn": gain_attn, "gain_mlp": gain_mlp, "cotangent": cotangent}


ROPE_BASE = 100000.0
EPS = 1e-05
PRECISE_MODE = lax.Precision.HIGHEST

@jax.custom_vjp
def low(v):
    return lax.optimization_barrier(v.astype(jnp.bfloat16)).astype(jnp.float32)

@jax.custom_vjp
def low_back(v):
    return v

def low_keep(v):
    return (low(v), None)

def low_pass(kept, grad):
    return (grad,)

def back_keep(v):
    return (v, None)

def back_low(kept, grad):
    return (low(grad),)
low.defvjp(low_keep, low_pass)
low_back.defvjp(back_keep, back_low)

def rope_tables(places):
    half_size = HD // 2
    inverse = ROPE_BASE ** (-jnp.arange(half_size).astype(jnp.float32) * 2.0 / HD)
    angles = places.astype(jnp.float32)[..., None] * inverse
    return (jnp.cos(angles), jnp.sin(angles))

def rotate(values, cosine, sine_table):
    half_size = values.shape[-1] // 2
    front_half = values[..., :half_size]
    back_half = values[..., half_size:]
    cos_part = cosine[..., None, :]
    sin_part = sine_table[..., None, :]
    return jnp.concatenate([front_half * cos_part - back_half * sin_part, back_half * cos_part + front_half * sin_part], axis=-1)

def rms_norm(values, gains):
    inv_scale = lax.rsqrt(lax.optimization_barrier(jnp.mean(values * values, axis=-1, keepdims=True)) + EPS)
    return values * inv_scale * gains

def project(input_tensor, weight_table):
    return jnp.einsum('ifk,kt->ift', input_tensor, weight_table, precision=PRECISE_MODE)

def attend(pieces):
    query_rows, key_rows, value_rows, places = pieces
    group_size = HQ // KVH
    keys_wide = jnp.repeat(key_rows, group_size, axis=1)
    values_wide = jnp.repeat(value_rows, group_size, axis=1)
    raw_scores = low_back(jnp.einsum('qhd,khd->hqk', query_rows, keys_wide, precision=PRECISE_MODE))
    scores = raw_scores * HD ** (-0.5)
    allowed = places[None, :] <= places[:, None]
    scores = jnp.where(allowed[None], scores, -1e+30)
    highest = lax.optimization_barrier(jnp.max(scores, axis=-1, keepdims=True))
    weights = jnp.exp(scores - highest)
    weights = weights / lax.optimization_barrier(jnp.sum(weights, axis=-1, keepdims=True))
    mixture = jnp.einsum('hqk,khd->qhd', low(weights), values_wide, precision=PRECISE_MODE)
    return low(low_back(mixture.reshape(mixture.shape[0], HQ * HD)))

def forward(tokens, w_query, w_key, w_value, w_out, w_gate, w_up, down_weight, gain_attn, gain_mlp, cosine, sine_table, positions):
    normed = low(rms_norm(tokens, gain_attn))
    query_all = project(normed, w_query).reshape(SEQS, LEN, HQ, HD)
    key_all = project(normed, w_key).reshape(SEQS, LEN, KVH, HD)
    value_all = project(normed, w_value).reshape(SEQS, LEN, KVH, HD)
    query_all = low(rotate(low_back(query_all), cosine, sine_table))
    key_all = low(rotate(low_back(key_all), cosine, sine_table))
    value_all = low(low_back(value_all))
    attended = lax.map(jax.checkpoint(attend), (query_all, key_all, value_all, positions))
    branch = low_back(project(attended, w_out))
    hidden = tokens + branch
    normed_mlp = low(rms_norm(hidden, gain_mlp))
    gate_lin = low_back(project(normed_mlp, w_gate))
    upward = low_back(project(normed_mlp, w_up))
    active = low(jax.nn.silu(gate_lin) * upward)
    return hidden + project(active, down_weight)

def reference(tokens, positions, w_query, w_key, w_value, w_out, w_gate, w_up, down_weight, gain_attn, gain_mlp, cotangent):
    cosine, sine_table = rope_tables(positions)
    floats = [array.astype(jnp.float32) for array in (tokens, w_query, w_key, w_value, w_out, w_gate, w_up, down_weight, gain_attn, gain_mlp)]

    def run_layer(*inputs):
        return forward(*inputs, cosine, sine_table, positions)
    output, pullback = jax.vjp(run_layer, *floats)
    gradients = pullback(cotangent.astype(jnp.float32))
    return (output.astype(jnp.bfloat16), gradients[0].astype(jnp.bfloat16), gradients[1], gradients[2], gradients[3], gradients[4], gradients[5], gradients[6], gradients[7], gradients[8], gradients[9])
```

```python
import functools
import math

import jax
import jax.numpy as jnp
from jax import lax
from jax.experimental import pallas as pl
from jax.experimental.pallas import tpu as pltpu
from jax.sharding import Mesh, PartitionSpec as P

HD = 96
PAD = 128
ROPE_BASE = 100000.0
EPS = 1e-05
MASKED_SCORE = -1e30
SCALE = HD**-0.5
LOG2E = math.log2(math.e)
BF = jnp.bfloat16
F32 = jnp.float32
Y = ("yl", "yh")
YZ = ("yl", "z", "yh")

ANY = pl.BlockSpec(memory_space=pl.ANY)
VM = pl.BlockSpec(memory_space=pltpu.VMEM)
SM = pl.BlockSpec(memory_space=pltpu.SMEM)


def after(v, *earlier):
    return lax.optimization_barrier((v,) + earlier)[0]


def all_after(pieces, *earlier):
    return list(lax.optimization_barrier(tuple(pieces) + earlier)[: len(pieces)])


def shift(v, axis, k):
    n = lax.axis_size(axis)
    name = [0, 2, 1, 3] if axis == Y else list(range(n))
    return lax.ppermute(v, axis, [(name[i], name[(i + k) % n]) for i in range(n)])


def around(v, axis):
    return [v] + [shift(v, axis, j) for j in range(1, lax.axis_size(axis))]


def send(pieces, axis, toward):
    return [pieces[0]] + [shift(pieces[j], axis, toward * j) for j in range(1, len(pieces))]


def add(pieces):
    total = pieces[0].astype(F32)
    for p in pieces[1:]:
        total = total + p.astype(F32)
    return total


def quarters(pieces):
    n = pieces[0].shape[0] // 4
    return [add([p[j * n : (j + 1) * n] for p in pieces]).astype(BF) for j in range(4)]


def nn(a, b):
    return lax.dot_general(a, b, (((1,), (0,)), ((), ())), preferred_element_type=F32)


def nt(a, b):
    return lax.dot_general(a, b, (((1,), (1,)), ((), ())), preferred_element_type=F32)


def kernel_call(us, body, outs, in_specs, out_specs, scratch, *args):
    return pl.pallas_call(
        body,
        out_shape=outs,
        in_specs=in_specs,
        out_specs=out_specs,
        scratch_shapes=scratch,
        compiler_params=pltpu.CompilerParams(vmem_limit_bytes=56 << 20),
        cost_estimate=pl.CostEstimate(
            flops=int(us * 1.1e9), transcendentals=0, bytes_accessed=int(us * 3.5e6)
        ),
    )(*args)


def struct(*shape, dtype=BF):
    return jax.ShapeDtypeStruct(shape, dtype)


def run(copies):
    for c in copies:
        c.start()
    for c in copies:
        c.wait()


def weighted(kernel):
    def body(at, *refs):
        kernel(at, refs[:4], refs[4:8], *refs[8:])

    return body


def weight_copies(at, own, other, held, sem, cut=None, steps=True):
    mx, mc, my = at[0], at[1], at[2]
    copies = []
    for c, refs in ((mc, own), (1 - mc, other)):
        for a in range(4):
            x = (mx - a + 4) & 3
            for b in range(4):
                y = (my - b + 4) & 3 if steps else (b & 1) * 2 + (b >> 1)
                row = pl.multiple_of(((x * 2 + c) * 2 + (y & 1)) * 96, 16)
                src = refs[a].at[b] if cut is None else refs[a].at[b, :, cut]
                copies.append(
                    pltpu.make_async_copy(src, held.at[y >> 1, pl.ds(row, 96)], sem.at[len(copies)])
                )
    return copies


def grad_copies(at, held, keep, give, sem, yh, x):
    mx, mc, my = at[0], at[1], at[2]
    a = (x - mx + 4) & 3
    copies = []
    for yl in range(2):
        b = yl * 2 + yh if isinstance(give, tuple) else (yh * 2 + yl - my + 4) & 3
        for r, (c, ref) in enumerate(((mc, keep), (1 - mc, give))):
            row = pl.multiple_of(((x * 2 + c) * 2 + yl) * 96, 16)
            src = held.at[yh, pl.ds(row, 96)]
            slot = sem.at[((yh * 4 + x) * 2 + yl) * 2 + r]
            if isinstance(ref, tuple):
                for k, row in ((2, 0), (1, 4), (3, 0), (0, 4)):
                    to = ref[0 if k in (1, 2) else 1].at[row + b]
                    copies.append((a == k, pltpu.make_async_copy(src, to, slot)))
            else:
                copies.append((None, pltpu.make_async_copy(src, ref.at[a * 4 + b], slot)))
    return copies


def each(copies, act):
    for when, c in copies:
        if when is None:
            act(c)
        else:
            pl.when(when)(functools.partial(act, c))


def start(c):
    c.start()


def wait(c):
    c.wait()


def wait_grads(at, held, keep, give, sem):
    for yh in range(2):
        for x in range(4):
            each(grad_copies(at, held, keep, give, sem, yh, x), wait)


def swap_halves(v):
    n = v.shape[1]
    lane = lax.broadcasted_iota(jnp.int32, v.shape, 1)
    for k in range(1, (n + HD - 1) // HD):
        lane = jnp.where(lane >= HD, lane - HD, lane)
    return jnp.where(lane < HD // 2, pltpu.roll(v, n - HD // 2, 1), pltpu.roll(v, HD // 2, 1))


def fill_rows(units, rows):
    for s in range(2):
        for yh in range(2):
            for j in range(4):
                rows[yh, j * 128 + s * 64 : j * 128 + s * 64 + 64] = units[
                    s * 2 + yh, j * 64 : (j + 1) * 64
                ]


def take_rows(v, yh, out):
    for j in range(4):
        for s in range(2):
            out[s * 2 + yh, j * 64 : (j + 1) * 64] = v[j * 128 + s * 64 : j * 128 + s * 64 + 64]


def piece_copies(pieces, rows, sem):
    return [
        pltpu.make_async_copy(p, rows.at[pl.ds(j * 128, 128)], sem.at[j]) for j, p in enumerate(pieces)
    ]


def qkv_kernel(at, own, other, n0, n1, n2, n3, cosine, sine, out, w, rows, sem, nsem):
    run(weight_copies(at, own, other, w, sem) + piece_copies((n0, n1, n2, n3), rows, nsem))
    for yh in range(2):
        v = nn(rows[...], w[yh])
        take_rows((v * cosine[...] + swap_halves(v) * sine[...]).astype(BF), yh, out)


def split_heads(unit):
    full = unit[...].reshape(1024, 384).astype(F32)
    lane = lax.broadcasted_iota(jnp.int32, (1024, PAD), 1)
    heads = []
    for h in range(4):
        v = full if h == 0 else pltpu.roll(full, 384 - HD * h, 1)
        heads.append(jnp.where(lane < HD, v[:, :PAD], 0.0))
    return heads


def attn_kernel(unit, pos_row, pos_col, out, lse, qs, ks, vt):
    q0, q1, k, v = split_heads(unit)
    qs[0], qs[1] = q0.astype(BF), q1.astype(BF)
    ks[...] = k.astype(BF)
    vt[...] = v.T.astype(BF)

    def block(b, _):
        cols = pl.ds(pl.multiple_of(b * 256, 256), 256)
        allowed = pos_col[...] <= pos_row[:, cols]
        for h in range(2):
            s = nt(ks[...], qs[h, cols]) * (SCALE * LOG2E)
            s = jnp.where(allowed, s, MASKED_SCORE)
            top = jnp.max(s, axis=0, keepdims=True)
            p = jnp.exp2(s - top)
            total = jnp.sum(p, axis=0, keepdims=True)
            o = nn(vt[...], p.astype(BF)) / total
            out[b, :, h * PAD : (h + 1) * PAD] = o.T.astype(BF)
            lse[h : h + 1, cols] = top + jnp.log2(total)
        return 0

    lax.fori_loop(0, 4, block, 0)


def attn_back_kernel(
    unit, g, pos_row, pos_col, lse, cosine, sine, out, qs, gs, ks, kt, vs, dq, dk, dv
):
    q0, q1, k, v = split_heads(unit)
    qs[0], qs[1] = q0.astype(BF), q1.astype(BF)
    ks[...] = k.astype(BF)
    kt[...] = k.T.astype(BF)
    vs[...] = v.astype(BF)
    for b in range(4):
        for h in range(2):
            gs[h, b * 256 : (b + 1) * 256] = g[b, :, h * PAD : (h + 1) * PAD]
    dk[...] = jnp.zeros_like(dk)
    dv[...] = jnp.zeros_like(dv)

    def block(b, _):
        cols = pl.ds(pl.multiple_of(b * 256, 256), 256)
        allowed = pos_col[...] <= pos_row[:, cols]
        for h in range(2):
            qb, gb = qs[h, cols], gs[h, cols]
            s = nt(ks[...], qb) * (SCALE * LOG2E)
            s = jnp.where(allowed, s, MASKED_SCORE)
            p = jnp.exp2(s - lse[h : h + 1, cols])
            dp = nt(vs[...], gb)
            inner = jnp.sum(p * dp, axis=0, keepdims=True)
            ds = (p * (dp - inner) * SCALE).astype(BF)
            dv[...] += nn(p.astype(BF), gb)
            dk[...] += nn(ds, qb)
            dq[h, cols] = nn(kt[...], ds).T
        return 0

    lax.fori_loop(0, 4, block, 0)

    def unrotate(v):
        return v * cosine[...] - swap_halves(v) * sine[...]

    blank = jnp.zeros((1024, 384 - PAD), F32)
    total = None
    for h, v in enumerate((unrotate(dq[0]), unrotate(dq[1]), unrotate(dk[...]), dv[...])):
        v = jnp.concatenate([v, blank], axis=1)
        v = v if h == 0 else pltpu.roll(v, HD * h, 1)
        total = v if total is None else total + v
    out[...] = total.astype(BF).reshape(4, 256, 384)


def out_kernel(at, own, other, home, out, w, rows, sem):
    copies = weight_copies(at, own, other, w, sem)
    for c in copies:
        c.start()
    fill_rows(home, rows)
    for c in copies:
        c.wait()
    for half in range(2):
        cut = slice(half * 256, (half + 1) * 256)
        got = (nt(rows[0, cut], w[0]) + nt(rows[1, cut], w[1])).astype(BF)
        for k in range(2):
            out[(at[3] - half * 2 - k + 4) & 3] = got[k * 128 : (k + 1) * 128]


def norm_kernel(parts, tokens, gain, hidden_out, m_out):
    hidden = tokens[...].astype(F32)
    for k in range(4):
        hidden = hidden + parts[k].astype(F32)
    inv = lax.rsqrt(jnp.mean(hidden * hidden, axis=-1, keepdims=True) + EPS)
    hidden_out[...] = hidden
    m_out[...] = (hidden * inv * gain[...]).astype(BF)


def mlp_kernel(n, at, own, other, *refs):
    m, c, g = refs[:n], refs[n : 2 * n], refs[2 * n : 3 * n]
    gain, act, w, ms, cs, total, sem, rsem, csem = refs[3 * n :]
    weights = weight_copies(at, own, other, w, sem, steps=False)
    pieces = piece_copies(m, ms, rsem) + piece_copies(c, cs, csem)
    for p in pieces + weights[0::2] + weights[1::2]:
        p.start()
    for p in pieces:
        p.wait()

    def part(yh):
        for p in weights[yh::2]:
            p.wait()
        gate = nn(ms[...], w[yh, :, 0:512])
        upward = nn(ms[...], w[yh, :, 512:1024])
        grad = nn(cs[...], w[yh, :, 1024:1536])
        sig = 1.0 / (1.0 + jnp.exp2(gate * -LOG2E))
        silu = gate * sig
        act[yh, :, 1024:1536] = (silu * upward).astype(BF)
        d_gate = (grad * upward * sig * (1.0 + gate * (1.0 - sig))).astype(BF)
        d_up = (grad * silu).astype(BF)
        act[yh, :, 0:512] = d_gate
        act[yh, :, 512:1024] = d_up
        got = nt(d_gate, w[yh, :, 0:512]) + nt(d_up, w[yh, :, 512:1024])

        total[...] = got if yh == 0 else total[...] + got

    part(0)
    part(1)
    for j, ref in enumerate(g):
        ref[...] = total[j * 128 : (j + 1) * 128].astype(BF)
    gain[...] = jnp.sum(total[...] * ms[...].astype(F32), axis=0, keepdims=True)


def mlp_grad_kernel(
    at,
    m0,
    m1,
    m2,
    m3,
    c0,
    c1,
    c2,
    c3,
    act0,
    act13,
    act2,
    keep,
    e0,
    e1,
    held,
    mt,
    ct,
    act,
    out_sem,
    act_sem,
):
    copies = [
        pltpu.make_async_copy(part.at[yh], act.at[yh, pl.ds(row, part.shape[1])], act_sem.at[row // 128, yh])
        for part, row in ((act0, 0), (act13, 128), (act2, 384))
        for yh in (0, 1)
    ]
    for c in copies:
        c.start()
    for j, (m, c) in enumerate(((m0, c0), (m1, c1), (m3, c3), (m2, c2))):
        mt[:, j * 128 : (j + 1) * 128] = m[...].astype(F32).T.astype(BF)
        ct[:, j * 128 : (j + 1) * 128] = c[...].astype(F32).T.astype(BF)

    for c in copies:
        c.wait()

    def part(t, _):
        yh, x = t & 1, t >> 1
        rows = pl.ds(pl.multiple_of(x * 384, 128), 384)
        held[yh, rows, 0:1024] = nn(mt[rows], act[yh, :, 0:1024]).astype(BF)
        held[yh, rows, 1024:1536] = nn(ct[rows], act[yh, :, 1024:1536]).astype(BF)
        each(grad_copies(at, held, keep, (e0, e1), out_sem, yh, x), start)
        return 0

    lax.fori_loop(0, 8, part, 0)
    wait_grads(at, held, keep, (e0, e1), out_sem)


def down_kernel(at, own, other, act0, act13, act2, d0, d1, d2, d3, w, sem):
    run(weight_copies(at, own, other, w, sem, pl.ds(1024, 512), False))
    for act, refs in ((act0, (d0,)), (act13, (d1, d3)), (act2, (d2,))):
        down = (nt(act[0, :, 1024:1536], w[0]) + nt(act[1, :, 1024:1536], w[1])).astype(BF)
        for k, ref in enumerate(refs):
            ref[...] = down[k * 128 : (k + 1) * 128]


def hidden_back_kernel(p0, p1, p2, p3, hidden, cot, gain, gh_out, ghb_out):
    up = p0[...].astype(F32) + p1[...].astype(F32) + p2[...].astype(F32) + p3[...].astype(F32)
    v = hidden[...]
    inv = lax.rsqrt(jnp.mean(v * v, axis=-1, keepdims=True) + EPS)
    weighted = up * gain[...]
    inner = jnp.sum(weighted * v, axis=-1, keepdims=True) * (1.0 / v.shape[-1])
    gh = cot[...].astype(F32) + inv * weighted - v * (inv * inv * inv * inner)
    gh_out[...] = gh
    ghb_out[...] = gh.astype(BF)


def out_back_kernel(at, own, other, h0, h1, h2, h3, out, w, rows, sem, hsem):
    run(weight_copies(at, own, other, w, sem) + piece_copies((h0, h1, h2, h3), rows, hsem))
    for yh in range(2):
        take_rows(nn(rows[...], w[yh]).astype(BF), yh, out)


def in_grad_kernel(at, out_w, n0, n1, n2, n3, g, keep, give, held, nt_rows, rows, out_sem, sem):
    copies = [
        pltpu.make_async_copy(out_w.at[yh], held.at[yh, :, pl.ds(384, 256)], sem.at[yh]) for yh in (0, 1)
    ]
    for c in copies:
        c.start()
    fill_rows(g, rows)
    for j, n in enumerate((n0, n1, n2, n3)):
        nt_rows[:, j * 128 : (j + 1) * 128] = n[...].astype(F32).T.astype(BF)
    for c in copies:
        c.wait()

    def part(t, _):
        yh, x = t & 1, t >> 1
        cut = pl.ds(pl.multiple_of(x * 384, 128), 384)
        held[yh, cut, 0:384] = nn(nt_rows[cut], rows[yh]).astype(BF)
        each(grad_copies(at, held, keep, give, out_sem, yh, x), start)
        return 0

    lax.fori_loop(0, 8, part, 0)
    wait_grads(at, held, keep, give, out_sem)


def out_grad_kernel(h0, h1, h2, h3, home, out, rows, cols):
    fill_rows(home, rows)
    for j, h in enumerate((h0, h1, h2, h3)):
        cols[:, j * 128 : (j + 1) * 128] = h[...].astype(F32).T.astype(BF)

    def part(x, _):
        cut = pl.ds(pl.multiple_of(x * 384, 128), 384)
        for yh in range(2):
            out[yh, cut] = nn(cols[cut], rows[yh]).astype(BF)
        return 0

    lax.fori_loop(0, 4, part, 0)


def normed_back_kernel(at, own, other, n0, n1, n2, n3, g, d0, d1, d2, d3, gain, w, rows, sem):
    copies = weight_copies(at, own, other, w, sem)
    for c in copies:
        c.start()
    fill_rows(g, rows)
    for c in copies:
        c.wait()
    total = jnp.zeros(gain.shape, F32)
    for half, (ns, refs) in enumerate((((n0, n1), (d0, d1)), ((n2, n3), (d2, d3)))):
        cut = slice(half * 256, (half + 1) * 256)
        got = nt(rows[0, cut], w[0]) + nt(rows[1, cut], w[1])
        for k in range(2):
            part = got[k * 128 : (k + 1) * 128]
            refs[k][...] = part.astype(BF)
            total = total + jnp.sum(part * ns[k][...].astype(F32), axis=0, keepdims=True)
    gain[...] = total


def rope_tables(places):
    half = HD // 2
    inverse = ROPE_BASE ** (-jnp.arange(half).astype(F32) * 2.0 / HD)
    angles = places.astype(F32)[..., None] * inverse
    c, s = jnp.cos(angles), jnp.sin(angles)
    return jnp.concatenate([c, c], axis=-1), jnp.concatenate([-s, s], axis=-1)


def everyone(v, axis):
    n = lax.axis_size(axis)
    wide = jnp.broadcast_to(v[None], (n,) + v.shape)
    return jnp.sum(lax.all_to_all(wide, axis, 0, 0, tiled=True), axis=0)


def dma(n):
    return pltpu.SemaphoreType.DMA((n,))


def shards(
    tokens,
    positions,
    w_query,
    w_key,
    w_value,
    w_out,
    w_gate,
    w_up,
    down_weight,
    gain_attn,
    gain_mlp,
    cotangent,
):
    seqs, rows, d = tokens.shape
    local = seqs * rows
    mx, mc, mz = lax.axis_index("x"), lax.axis_index("core"), lax.axis_index("z")
    yl, yh = lax.axis_index("yl"), lax.axis_index("yh")
    my = yh * 2 + yl
    at = jnp.stack([mx, mc, my, mz]).astype(jnp.int32)
    src_z = (mz - jnp.arange(4)) % 4
    gain_m = gain_mlp.reshape(1, d)
    out_t = jnp.pad(w_out.T.reshape(96, 2, HD), ((0, 0), (0, 0), (0, PAD - HD))).reshape(96, 256)
    in_pack = jnp.concatenate([w_query, w_key, w_value, out_t], axis=1)

    rows_in = tokens.reshape(local, d)
    stream = rows_in.astype(F32)
    cot = cotangent.reshape(local, d)
    inv_first = lax.rsqrt(jnp.mean(stream * stream, axis=-1, keepdims=True) + EPS)
    normed = (stream * inv_first * gain_attn).astype(BF)
    in_y = all_after(around(in_pack, Y), normed)
    in_y, out_y = jnp.stack([p[:, :384] for p in in_y]), jnp.stack([p[:, 384:] for p in in_y])

    places = positions.reshape(seqs, 2, 4, 2, rows).transpose(0, 1, 3, 2, 4)
    places = places.reshape(seqs, 4, 4, rows)[:, :, src_z]
    mine = lax.dynamic_index_in_dim(places, yl * 2 + yh, 1, keepdims=False)
    mine = mine.transpose(1, 0, 2).reshape(4 * local)
    unit_places = lax.dynamic_index_in_dim(places, yl, 0, keepdims=False).reshape(-1)
    c, s = rope_tables(mine)
    cosine = jnp.concatenate([c, c, c, jnp.ones_like(c)], axis=-1)
    sine = jnp.concatenate([s, s, s, jnp.zeros_like(s)], axis=-1)
    c, s = rope_tables(unit_places)
    unit_cos = jnp.pad(c, ((0, 0), (0, PAD - HD)))
    unit_sin = jnp.pad(s, ((0, 0), (0, PAD - HD)))
    pos_row, pos_col = unit_places.reshape(1, -1), unit_places.reshape(-1, 1)

    def to_other(pieces):
        return list(pieces) + [shift(p, "core", 1) for p in pieces]

    n2, n3 = shift(normed, "z", 2), shift(normed, "z", 3)
    in_x = around(in_y, "x")
    n1 = shift(after(normed, in_x[1]), "z", 1)
    in_x = in_x[:1] + all_after(in_x[1:], n2, n3, cosine, sine)
    n_pieces = [normed, n1, n2, n3]
    in_w = to_other(in_x)
    mlp_pack = all_after([w_gate, w_up, down_weight], n3)
    mlp_pack = jnp.concatenate([mlp_pack[0], mlp_pack[1], mlp_pack[2].T], axis=1)
    mlp_y = jnp.broadcast_to(mlp_pack[None], (4,) + mlp_pack.shape)
    mlp_y = lax.all_to_all(mlp_y, Y, 0, 0, tiled=True)

    to_unit = kernel_call(
        0,
        weighted(qkv_kernel),
        struct(4, 256, 384),
        [SM] + [ANY] * 12 + [VM] * 2,
        VM,
        [pltpu.VMEM((2, d, 384), BF), pltpu.VMEM((512, d), BF), dma(32), dma(4)],
        at,
        *in_w,
        *n_pieces,
        cosine,
        sine,
    )
    unit = lax.all_to_all(to_unit, Y, 0, 0, tiled=True)
    out_x = around(after(out_y, in_w[5]), "x")
    cot1, cot3 = [shift(after(cot, n2), "z", k) for k in (1, 3)]
    mlp_y = after(mlp_y, *out_x[1:])
    mlp1, mlp3 = shift(mlp_y, "x", 1), shift(mlp_y, "x", 3)
    mlp2 = shift(after(mlp_y, to_unit), "x", 2)
    unit = after(unit, *out_x[1:])
    mixed, lse = kernel_call(
        0,
        attn_kernel,
        [struct(4, 256, 256), struct(2, 1024, dtype=F32)],
        [VM] * 3,
        [VM] * 2,
        [pltpu.VMEM((2, 1024, PAD), BF), pltpu.VMEM((1024, PAD), BF), pltpu.VMEM((PAD, 1024), BF)],
        unit,
        pos_row,
        pos_col,
    )
    mixed = after(mixed, cot1, cot3)
    home = lax.all_to_all(mixed, Y, 0, 0, tiled=True)
    out_w = to_other(all_after(out_x, mixed))
    cot2 = shift(after(cot, mixed), "z", 2)
    home, cot2 = all_after([home, cot2])
    cot_pieces = [cot, cot1, cot2, cot3]
    branch = kernel_call(
        0,
        weighted(out_kernel),
        struct(4, local, d),
        [SM] + [ANY] * 8 + [VM],
        VM,
        [pltpu.VMEM((2, d, 256), BF), pltpu.VMEM((2, 512, 256), BF), dma(32)],
        at,
        *out_w,
        home,
    )
    mlp_other = [shift(p, "core", 1) for p in all_after([mlp_y, mlp1, mlp3], branch)]
    branch = lax.all_to_all(branch, "z", 0, 0, tiled=True)
    branch, mlp2 = all_after([branch, mlp2], unit_cos, unit_sin, *mlp_other)
    hidden, normed_mlp = kernel_call(
        0,
        norm_kernel,
        [struct(local, d, dtype=F32), struct(local, d)],
        [VM] * 3,
        [VM] * 2,
        [],
        branch,
        rows_in,
        gain_m,
    )
    m1, m3 = shift(normed_mlp, "z", 1), shift(normed_mlp, "z", 3)
    m_pieces = [normed_mlp, m1, None, m3]
    mlp_w = [mlp_y, mlp1, mlp2, mlp3] + mlp_other[:2] + [shift(mlp2, "core", 1), mlp_other[2]]

    def feed_forward(us, order, *earlier):
        n = len(order)
        return kernel_call(
            us,
            weighted(functools.partial(mlp_kernel, n)),
            [struct(local, d)] * n + [struct(1, d, dtype=F32), struct(2, 128 * n, 1536)],
            [SM] + [ANY] * (8 + 2 * n),
            [VM] * (n + 2),
            [
                pltpu.VMEM((2, d, 1536), BF),
                pltpu.VMEM((128 * n, d), BF),
                pltpu.VMEM((128 * n, d), BF),
                pltpu.VMEM((128 * n, d), F32),
                dma(32),
                dma(n),
                dma(n),
            ],
            at,
            *mlp_w,
            *all_after([m_pieces[k] for k in order], *earlier),
            *[cot_pieces[k] for k in order],
        )

    g_own, terms0, act0 = feed_forward(8, (0,), normed_mlp)
    m_pieces[2] = shift(after(normed_mlp, m1, act0), "z", 2)
    g_z1, g_z3, terms13, act13 = feed_forward(0, (1, 3), act0)
    g_z1, g_z3 = shift(g_z1, "z", -1), shift(g_z3, "z", -3)
    g_z2, terms2, act2 = feed_forward(8, (2,), act13)
    g_got = [g_own, g_z1, shift(after(g_z2, g_z1, g_z3), "z", -2), g_z3]
    terms_mlp = terms0 + terms13 + terms2
    mlp_keep, *mlp_give = kernel_call(
        13,
        mlp_grad_kernel,
        [struct(16, 96, 1536)] + [struct(8, 96, 1536)] * 2,
        [SM] + [VM] * 8 + [ANY] * 3,
        [ANY] * 3,
        [
            pltpu.VMEM((2, d, 1536), BF),
            pltpu.VMEM((d, 512), BF),
            pltpu.VMEM((d, 512), BF),
            pltpu.VMEM((2, 512, 1536), BF),
            dma(32),
            pltpu.SemaphoreType.DMA((4, 2)),
        ],
        at,
        *m_pieces,
        *cot_pieces,
        act0,
        act13,
        act2,
    )
    g_got = all_after(g_got, mlp_keep)

    grad_hidden, g_hidden = kernel_call(
        0,
        hidden_back_kernel,
        [struct(local, d, dtype=F32), struct(local, d)],
        [VM] * 7,
        [VM] * 2,
        [],
        *g_got,
        hidden,
        cot,
        gain_m,
    )
    h_pieces = around(g_hidden, "z")
    down = kernel_call(
        4,
        weighted(down_kernel),
        [struct(local, d)] * 4,
        [SM] + [ANY] * 8 + [VM] * 3,
        [VM] * 4,
        [pltpu.VMEM((2, d, 512), BF), dma(32)],
        at,
        *mlp_w,
        act0,
        act13,
        after(act2, g_hidden),
    )
    mlp_got = [shift(p, "core", 1) for p in all_after(mlp_give, g_got[1])]

    def mlp_part(j, half):
        kept, got = j * 4 + half * 2, (4, 4, 0, 0)[j] + half * 2
        other = mlp_got[(1, 0, 0, 1)[j]][got : got + 2]
        return add([mlp_keep[kept : kept + 2], other]).astype(BF)

    mlp_got = all_after(mlp_got, down[0])
    relay = [mlp_part(2, 0), mlp_part(2, 1)]
    g_out = kernel_call(
        0,
        weighted(out_back_kernel),
        struct(4, 256, 256),
        [SM] + [ANY] * 12,
        VM,
        [pltpu.VMEM((2, d, 256), BF), pltpu.VMEM((512, d), BF), dma(32), dma(4)],
        at,
        *out_w,
        *all_after(h_pieces, *relay),
    )
    g_mix = lax.all_to_all(g_out, Y, 0, 0, tiled=True)
    grad_out = kernel_call(
        5,
        out_grad_kernel,
        struct(2, d, 256),
        [VM] * 5,
        VM,
        [pltpu.VMEM((2, 512, 256), BF), pltpu.VMEM((d, 512), BF)],
        *h_pieces,
        after(home, g_out),
    )
    relay = [shift(relay[0], "x", 1), shift(relay[1], "x", -1)]
    down = send(all_after(down, h_pieces[1]), "z", -1)
    g_mix = after(g_mix, grad_out, *relay, *down[1:])
    relay = all_after(relay, g_mix)
    relay = [
        jnp.concatenate([add([mlp_part(1, 0), relay[0]]).astype(BF), mlp_part(1, 1)]),
        jnp.concatenate([mlp_part(3, 0), add([mlp_part(3, 1), relay[1]]).astype(BF)]),
    ]
    g_mix = after(g_mix, *relay)
    relay = [shift(relay[0], "x", 1), shift(relay[1], "x", -1)]
    g_unit = kernel_call(
        0,
        attn_back_kernel,
        struct(4, 256, 384),
        [VM] * 7,
        VM,
        [
            pltpu.VMEM((2, 1024, PAD), BF),
            pltpu.VMEM((2, 1024, PAD), BF),
            pltpu.VMEM((1024, PAD), BF),
            pltpu.VMEM((PAD, 1024), BF),
            pltpu.VMEM((1024, PAD), BF),
            pltpu.VMEM((2, 1024, PAD), F32),
            pltpu.VMEM((1024, PAD), F32),
            pltpu.VMEM((1024, PAD), F32),
        ],
        unit,
        g_mix,
        pos_row,
        pos_col,
        lse,
        unit_cos,
        unit_sin,
    )
    g_qkv = lax.all_to_all(g_unit, Y, 0, 0, tiled=True)
    relay = all_after(relay, g_unit)
    mlp_sum = [add([mlp_part(0, k), relay[0][2 * k : 2 * k + 2], relay[1][2 * k : 2 * k + 2]]) for k in (0, 1)]
    mlp_sum = jnp.concatenate(mlp_sum).astype(BF)
    g_qkv = after(g_qkv, mlp_sum)
    mlp_got = lax.all_to_all(mlp_sum, Y, 0, 0, tiled=True)
    in_keep, in_give = kernel_call(
        0,
        in_grad_kernel,
        [struct(16, 96, 640)] * 2,
        [SM, ANY] + [VM] * 5,
        [ANY] * 2,
        [
            pltpu.VMEM((2, d, 640), BF),
            pltpu.VMEM((d, 512), BF),
            pltpu.VMEM((2, 512, 384), BF),
            dma(32),
            dma(2),
        ],
        at,
        grad_out,
        *n_pieces,
        g_qkv,
    )
    in_got = shift(in_give, "core", 1)
    in_parts = quarters([in_keep, in_got])
    *g_norm, terms_attn = kernel_call(
        6,
        weighted(normed_back_kernel),
        [struct(local, d)] * 4 + [struct(1, d, dtype=F32)],
        [SM] + [ANY] * 8 + [VM] * 5,
        [VM] * 5,
        [pltpu.VMEM((2, d, 384), BF), pltpu.VMEM((2, 512, 384), BF), dma(32)],
        at,
        *in_w,
        *n_pieces,
        after(g_qkv, in_parts[0]),
    )
    in_parts = send(in_parts, "x", 1)
    gains = jnp.concatenate([terms_attn, terms_mlp])
    gains = everyone(after(gains, mlp_got, g_norm[0]), ("x", "core"))
    g_norm1, g_norm3 = shift(g_norm[1], "z", -1), shift(g_norm[3], "z", -3)
    in_parts = quarters(all_after(in_parts, g_norm1, g_norm3, gains))
    g_norm = [g_norm[0], g_norm1, shift(after(g_norm[2], in_parts[0]), "z", -2), g_norm3]
    in_parts = send(in_parts, Y, 1)
    gains = everyone(after(gains, in_parts[1]), YZ)
    in_parts = all_after(in_parts, g_norm[2])
    up = add(g_norm) * gain_attn
    inner = jnp.sum(up * stream, axis=-1, keepdims=True) / d
    grad_stream = inv_first * up - stream * inv_first**3 * inner
    grad_tokens = (grad_hidden + grad_stream).astype(BF)
    output = (hidden + add(all_after(down, in_parts[0]))).astype(BF)
    grad_w_mlp = jnp.sum(mlp_got.astype(F32), axis=0)
    grad_w_in, grad_w_out = add(in_parts)[0][:, :384], add(in_parts)[0][:, 384:]
    grad_w_out = grad_w_out.reshape(96, 2, PAD)[..., :HD].reshape(96, 2 * HD)
    return (
        output.reshape(tokens.shape),
        grad_tokens.reshape(tokens.shape),
        grad_w_in[:, :192],
        grad_w_in[:, 192:288],
        grad_w_in[:, 288:],
        grad_w_out.T,
        grad_w_mlp[:, :512],
        grad_w_mlp[:, 512:1024],
        grad_w_mlp[:, 1024:].T,
        gains[0] / gain_attn,
        gains[1] / gain_mlp,
    )


def solution(mesh):
    fine = Mesh(mesh.devices.reshape(4, 2, 2, 4, 2), ("x", "core", "yl", "z", "yh"))
    acts = P(("x", "core"), ("yl", "z", "yh"), None)
    by_row = P(("x", "core", "yl"), ("z", "yh"))
    by_col = P(("z", "yh"), ("x", "core", "yl"))
    in_specs = (
        acts,
        P(("x", "core"), None),
        by_row,
        by_row,
        by_row,
        by_col,
        by_row,
        by_row,
        by_col,
        P(),
        P(),
        acts,
    )
    out_specs = (acts, acts, by_row, by_row, by_row, by_col, by_row, by_row, by_col, P(), P())
    return jax.shard_map(shards, mesh=fine, in_specs=in_specs, out_specs=out_specs, check_vma=False)
```
